256 devices in a mesh: head: 8 (over y, core), seq: 32 (over z, x).
Axes of the slice: x: 4, y: 4, z: 8, core: 2. Of those that a mesh axis runs over, the one named last changes fastest.
Arguments:
- queries: bfloat16 [32768, 2048], P('seq', 'head'), may hold values from -4 to 4
- keys: bfloat16 [32768, 2048], P('seq', 'head'), may hold values from -4 to 4
- values: bfloat16 [32768, 4096], P('seq', 'head'), may hold values from -6 to 6
- input_gate: float32 [32768, 8], P('seq', 'head'), may hold values from -4 to 4
- forget_gate: float32 [32768, 8], P('seq', 'head')
- out_weight: bfloat16 [4096, 4096], P('head', 'seq'), may hold values from -0.09375 to 0.09375
Outputs:
- mixed: bfloat16 [32768, 4096], P('seq', 'head')
The draws below stay inside these ranges and needn't reach their ends.
All inputs are finite; a program needn't handle non-finite values.
Results may differ from the reference program's by a relative error of at most 0.019.
Values may be sent and summed in bfloat16 or wider, within the bound.
A program may use at most 128 MiB of HBM per device.

```python
import math
import jax
import jax.numpy as jnp
from jax import lax

D = 4096
HEAD_TOTAL = 8
DK = 256
DV = 512
WINDOW = 1024
TOK_DEV = 1024
TOKEN_TOTAL = 32768


def paired_rows(key):
    random_keys_list = jax.random.split(jax.random.fold_in(key, 11), 3)
    row_count = TOKEN_TOTAL
    col_count = HEAD_TOTAL * DK
    query_rows = jnp.clip(jax.random.normal(random_keys_list[1], (row_count, col_count)), -4.0, 4.0)
    key_rows = jnp.clip(jax.random.normal(random_keys_list[2], (row_count, col_count)), -4.0, 4.0)
    return (query_rows, key_rows)


def draw_queries(key, part):
    return paired_rows(key)[0].astype(jnp.bfloat16)


def draw_keys(key, part):
    return paired_rows(key)[1].astype(jnp.bfloat16)


def draw_forget_gate(key, part):
    random_keys_list = jax.random.split(jax.random.fold_in(key, 23), 7)
    ranks = jax.random.permutation(random_keys_list[0], HEAD_TOTAL)
    slow_count = HEAD_TOTAL // 2
    slow = ranks < slow_count
    offset = jax.random.uniform(random_keys_list[1], (HEAD_TOTAL,))
    memory_length = jax.random.uniform(random_keys_list[2], (HEAD_TOTAL,), minval=30.0, maxval=50.0)
    baseline_gate_level = jnp.where(slow, math.log(TOKEN_TOTAL) + 1.3 + offset, jnp.log(memory_length))
    token_positions = jnp.arange(TOKEN_TOTAL)
    partition_gate_level = jax.random.uniform(random_keys_list[3], (TOKEN_TOTAL // TOK_DEV, HEAD_TOTAL), minval=-0.7, maxval=0.0)[token_positions // TOK_DEV]
    gate_jitter = jax.random.uniform(random_keys_list[4], (TOKEN_TOTAL, HEAD_TOTAL), minval=-0.35, maxval=0.35)
    spike_position = jax.random.randint(random_keys_list[5], (3, HEAD_TOTAL), 0, TOKEN_TOTAL)
    spike_enabled = jnp.any(token_positions[:, None, None] == spike_position[None, :, :], axis=1)
    spike_gate_level = jax.random.uniform(random_keys_list[6], (TOKEN_TOTAL, HEAD_TOTAL), minval=math.log(0.65 / 0.35), maxval=math.log(4.0))
    return jnp.where(spike_enabled, spike_gate_level, baseline_gate_level[None, :] + partition_gate_level + gate_jitter).astype(jnp.float32)


def block_scale(own_key, extent, cuts, least, high):
    loudness = 1.0
    for axis_at, shards_of in cuts:
        heights = jax.random.uniform(jax.random.fold_in(jax.random.fold_in(own_key, 6), axis_at), (shards_of,), jnp.float32, least / len(cuts), high / len(cuts))
        loudness = loudness * jnp.repeat(jnp.exp(heights), extent[axis_at] // shards_of).reshape((-1,) + (1,) * (len(extent) - 1 - axis_at))
    return loudness


def scatter_about(rng, dims, spread, most, shards=(), kind=jnp.bfloat16):
    loudness = block_scale(rng, dims, shards, -0.22, 0.18) if shards else 1.0
    drawn = jax.random.normal(rng, dims, jnp.float32) * spread * loudness
    return jnp.minimum(jnp.maximum(drawn, -most), most).astype(kind)


def setup_inputs(seed: int = 0) -> dict:
    key_list = jax.random.split(jax.random.key(seed), 7)
    return {
        "queries": draw_queries(jax.random.fold_in(key_list[6], 71), 0),
        "keys": draw_keys(jax.random.fold_in(key_list[6], 71), 0),
        "values": scatter_about(key_list[2], (TOKEN_TOTAL, HEAD_TOTAL * DV), 1.0, 6.0, ((0, 32), (1, 8))),
        "input_gate": scatter_about(key_list[3], (TOKEN_TOTAL, HEAD_TOTAL), 1.0, 4.0, ((0, 32), (1, 8)), jnp.float32),
        "forget_gate": draw_forget_gate(jax.random.fold_in(key_list[6], 71), 0),
        "out_weight": scatter_about(key_list[5], (HEAD_TOTAL * DV, D), (HEAD_TOTAL * DV) ** -0.5, 0.09375, ((0, 8), (1, 32))),
    }


PRECISE = lax.Precision.HIGHEST
VERY_NEGATIVE = -1e30


def memory_block(query_rows, key_rows, value_rows, gate_keys, cum_query, cum_key, first_row, carry_state):
    mem_c, mem_n, mem_m = carry_state
    key_scale = query_rows.shape[-1] ** -0.5
    scores = jnp.dot(query_rows, key_rows.T, preferred_element_type=jnp.float32) * key_scale
    query_index = first_row + jnp.arange(query_rows.shape[0], dtype=jnp.int32)
    key_index = jnp.arange(key_rows.shape[0], dtype=jnp.int32)
    causal = key_index[None, :] <= query_index[:, None]
    log_decay = jnp.where(causal, cum_query[:, None] - cum_key[None, :] + gate_keys[None, :], VERY_NEGATIVE)
    carry_log = cum_query + mem_m
    mem_max = jnp.maximum(jnp.max(log_decay, axis=1), carry_log)
    decays = jnp.where(causal, jnp.exp(log_decay - mem_max[:, None]), 0.0)
    weighted = decays * scores
    carry_scale = jnp.exp(carry_log - mem_max)
    query_full = query_rows.astype(jnp.float32) * key_scale
    numerator = jnp.dot(weighted.astype(jnp.bfloat16), value_rows, preferred_element_type=jnp.float32)
    numerator = numerator + carry_scale[:, None] * jnp.dot(query_full, mem_c, precision=PRECISE)
    denominator = jnp.sum(weighted, axis=1) + carry_scale * jnp.dot(query_full, mem_n, precision=PRECISE)
    return numerator, denominator, mem_max


def window_block(query_rows, key_window, value_window, query_pos, key_pos, mem_max):
    key_scale = query_rows.shape[-1] ** -0.5
    scores = jnp.dot(query_rows, key_window.T, preferred_element_type=jnp.float32) * key_scale
    visible = (key_pos[None, :] <= query_pos[:, None]) & (key_pos[None, :] > query_pos[:, None] - WINDOW) & (key_pos[None, :] >= 0)
    top_score = jnp.max(jnp.where(visible, scores, VERY_NEGATIVE), axis=1)
    joint_max = jnp.maximum(top_score, mem_max)
    weights = jnp.where(visible, jnp.exp(scores - joint_max[:, None]), 0.0)
    numerator = jnp.dot(weights.astype(jnp.bfloat16), value_window, preferred_element_type=jnp.float32)
    return numerator, jnp.sum(weights, axis=1), joint_max


def joint_output(window, memory):
    win_num, win_den, joint_max = window
    mem_num, mem_den, mem_max = memory
    lifted = jnp.exp(mem_max - joint_max)
    bottom = win_den + lifted * jnp.maximum(jnp.abs(mem_den), 1.0)
    return ((win_num + lifted[:, None] * mem_num) / bottom[:, None]).astype(jnp.bfloat16)


def span_summary(key_rows, value_rows, gate_keys, cum_key):
    total_decay = cum_key[-1]
    log_weight = total_decay - cum_key + gate_keys
    new_max = jnp.max(log_weight)
    scaled_keys = key_rows.astype(jnp.float32) * jnp.exp(log_weight - new_max)[:, None]
    mem_c = jnp.dot(scaled_keys.T, value_rows.astype(jnp.float32), precision=PRECISE)
    return mem_c, jnp.sum(scaled_keys, axis=0), new_max, total_decay


def merge_states(older, newer):
    lifted = newer[3] + older[2]
    new_max = jnp.maximum(lifted, newer[2])
    old_weight = jnp.exp(lifted - new_max)
    new_weight = jnp.exp(newer[2] - new_max)
    mem_c = old_weight[..., None, None] * older[0] + new_weight[..., None, None] * newer[0]
    mem_n = old_weight[..., None] * older[1] + new_weight[..., None] * newer[1]
    return mem_c, mem_n, new_max, older[3] + newer[3]


def head_reference(query_all, key_all, value_all, gate_all, forget_all):
    row_count = query_all.shape[0]
    block_rows = min(TOK_DEV, 512)
    block_count = row_count // block_rows
    padded_keys = jnp.concatenate([jnp.zeros((WINDOW, key_all.shape[1]), key_all.dtype), key_all], axis=0)
    padded_values = jnp.concatenate([jnp.zeros((WINDOW, value_all.shape[1]), value_all.dtype), value_all], axis=0)
    log_forget = jax.nn.log_sigmoid(forget_all)

    def block_step(carry_state, block_index):
        start_row = (block_index * block_rows).astype(jnp.int32)
        query_rows = lax.dynamic_slice_in_dim(query_all, start_row, block_rows)
        key_rows = lax.dynamic_slice_in_dim(key_all, start_row, block_rows)
        value_rows = lax.dynamic_slice_in_dim(value_all, start_row, block_rows)
        gate_keys = lax.dynamic_slice_in_dim(gate_all, start_row, block_rows)
        cum_gate = jnp.cumsum(lax.dynamic_slice_in_dim(log_forget, start_row, block_rows))
        memory = memory_block(query_rows, key_rows, value_rows, gate_keys, cum_gate, cum_gate, 0, carry_state[:3])
        key_window = lax.dynamic_slice_in_dim(padded_keys, start_row, WINDOW + block_rows)
        value_window = lax.dynamic_slice_in_dim(padded_values, start_row, WINDOW + block_rows)
        query_pos = start_row + jnp.arange(block_rows, dtype=jnp.int32)
        key_pos = start_row - WINDOW + jnp.arange(WINDOW + block_rows, dtype=jnp.int32)
        window = window_block(query_rows, key_window, value_window, query_pos, key_pos, memory[2])
        result = joint_output(window, memory)
        updated = merge_states(carry_state, span_summary(key_rows, value_rows, gate_keys, cum_gate))
        return updated, result

    initial = (jnp.zeros((DK, DV), jnp.float32), jnp.zeros((DK,), jnp.float32), jnp.array(VERY_NEGATIVE, jnp.float32), jnp.array(0.0, jnp.float32))
    _, results = lax.scan(block_step, initial, jnp.arange(block_count, dtype=jnp.int32))
    return results.reshape(row_count, DV)


def reference(queries, keys, values, input_gate, forget_gate, out_weight):
    query_heads = queries.reshape(TOKEN_TOTAL, HEAD_TOTAL, DK).transpose(1, 0, 2)
    key_heads = keys.reshape(TOKEN_TOTAL, HEAD_TOTAL, DK).transpose(1, 0, 2)
    value_heads = values.reshape(TOKEN_TOTAL, HEAD_TOTAL, DV).transpose(1, 0, 2)
    hidden = lax.map(lambda entry: head_reference(*entry), (query_heads, key_heads, value_heads, input_gate.T, forget_gate.T))
    hidden = hidden.transpose(1, 0, 2).reshape(TOKEN_TOTAL, HEAD_TOTAL * DV)
    return jnp.dot(hidden, out_weight, preferred_element_type=jnp.float32).astype(jnp.bfloat16)
```

```python
import functools

import jax
import jax.numpy as jnp
from jax import lax
from jax.experimental import pallas as pl
from jax.experimental.pallas import tpu as pltpu
from jax.sharding import PartitionSpec as P

MESH = pl.DeviceIdType.MESH
NEG = -1e30
F32 = jnp.float32
BF16 = jnp.bfloat16

ROWS = 1024
DK = 256
DV = 512
CH = 256
NCH = ROWS // CH
HEADS = 8
SEQ = 32
NZ = 8
NX = 4
SL = 16


def nt(a, b):
    return lax.dot_general(a, b, (((1,), (1,)), ((), ())), preferred_element_type=F32)


def nn(a, b):
    return jnp.dot(a, b, preferred_element_type=F32)


def kernel(
    q_ref, k_ref, v_ref, ig_ref, fg_ref, w_ref, out_ref,
    kp, vp, wbuf, hid, num, cflat, crecv, csend, cpre, meta,
    cumc, mml, xs, aw, bw, carried,
    kv_s, kv_r, w0_s, w0_r, wx_s, wx_r, wz_s, wz_r, sc_s, sc_r, h_s, h_r,
):
    h = lax.axis_index("head")
    s = lax.axis_index("seq")
    z, x = s // NX, s % NX
    y, core = h // 2, h % 2
    mate = y * 2 + (1 - core)
    up = ((y + 1) % 4) * 2 + core
    down = ((y + 3) % 4) * 2 + core
    across = ((y + 2) % 4) * 2 + core
    z_up = ((z + 1) % NZ) * NX + x
    z_down = ((z + NZ - 1) % NZ) * NX + x

    def remote(src, dst, ss, rs, dev):
        return pltpu.make_async_remote_copy(
            src_ref=src, dst_ref=dst, send_sem=ss, recv_sem=rs, device_id=dev, device_id_type=MESH
        )

    barrier = pltpu.get_barrier_semaphore()

    def greet(dev):
        pl.semaphore_signal(barrier, inc=1, device_id=dev, device_id_type=MESH)

    def greet_seq(k, c):
        greet((h, (s + k) % SEQ))
        return c

    lax.fori_loop(1, SEQ, greet_seq, 0)
    greet((mate, s))
    greet((up, s))
    greet((down, s))
    off_diag = z != h

    @pl.when(off_diag)
    def _():
        greet((z, h * NX + x))

    pl.semaphore_wait(barrier, SEQ - 1 + 3 + jnp.where(off_diag, 1, 0))

    def kv_copies(c):
        rows = pl.ds(c * CH, CH)
        to = (h, (s + 1) % SEQ)
        return (
            remote(k_ref.at[rows], kp.at[rows], kv_s.at[c, 0], kv_r.at[c, 0], to),
            remote(v_ref.at[rows], vp.at[rows], kv_s.at[c, 1], kv_r.at[c, 1], to),
        )

    for c in reversed(range(NCH)):
        for d in kv_copies(c):
            d.start()

    def w_block(row_block, col):
        return wbuf.at[row_block, :, pl.ds(pl.multiple_of(col * 128, 128), 128)]

    w0 = remote(w_ref, w_block(h, x), w0_s, w0_r, (z, h * NX + x))

    @pl.when(off_diag)
    def _():
        w0.start()

    @pl.when(jnp.logical_not(off_diag))
    def _():
        wbuf[z, :, pl.ds(pl.multiple_of(x * 128, 128), 128)] = w_ref[...]

    f_row = fg_ref[...]
    lf = jnp.minimum(f_row, 0.0) - jnp.log1p(jnp.exp(-jnp.abs(f_row)))
    lf8 = jnp.concatenate([lf[:, k * 128 : (k + 1) * 128] for k in range(8)], axis=0)
    tri = (
        lax.broadcasted_iota(jnp.int32, (128, 128), 0)
        <= lax.broadcasted_iota(jnp.int32, (128, 128), 1)
    ).astype(F32)
    part = jnp.dot(lf8, tri, precision=lax.Precision.HIGHEST, preferred_element_type=F32)
    pieces = []
    offset = jnp.zeros((1, 1), F32)
    for k in range(8):
        pieces.append(part[k : k + 1, :] + offset)
        offset = offset + part[k : k + 1, 127:128]
    cum_row = jnp.concatenate(pieces, axis=1)
    total = offset
    u_row = ig_ref[...] - cum_row
    u_max = jnp.max(u_row, axis=1, keepdims=True)
    w_row = jnp.exp(u_row - u_max)
    cumc[...] = jnp.transpose(jnp.broadcast_to(cum_row, (128, ROWS)))
    w_col = jnp.transpose(jnp.broadcast_to(w_row, (128, ROWS)))[:, 0:1]

    kw = k_ref[...].astype(F32) * w_col
    n_own = jnp.sum(kw, axis=0, keepdims=True)
    kw_t = jnp.transpose(kw).astype(BF16)
    cflat[0:DK, :] = nn(kw_t, v_ref[:, 0 : DV // 2]).astype(BF16)
    cflat[DK : 2 * DK, :] = nn(kw_t, v_ref[:, DV // 2 : DV]).astype(BF16)
    meta[s] = jnp.concatenate(
        [
            jnp.broadcast_to(total, (1, 128)),
            jnp.broadcast_to(total + u_max, (1, 128)),
            n_own[:, 0:128],
            n_own[:, 128:256],
            jnp.zeros((4, 128), F32),
        ],
        axis=0,
    )

    def piece(i):
        return pl.ds(pl.multiple_of(i * SL, SL), SL)

    def send_meta(k, c):
        to = (s + k) % SEQ
        remote(meta.at[s], meta.at[s], sc_s.at[0], sc_r.at[0], (h, to)).start()
        remote(cflat.at[piece(to)], crecv.at[piece(s)], sc_s.at[1], sc_r.at[1], (h, to)).start()
        return c

    lax.fori_loop(1, SEQ, send_meta, 0)
    crecv[piece(s), :] = cflat[piece(s), :]

    def chunk_own(i):
        rows = pl.ds(i * CH, CH)
        nk = (i + 1) * CH
        q = q_ref[rows] * BF16(DK**-0.5)
        sc = nt(q, k_ref[0:nk, :])
        mask = lax.broadcasted_iota(jnp.int32, (CH, nk), 1) <= (
            lax.broadcasted_iota(jnp.int32, (CH, nk), 0) + i * CH
        )
        cum = cumc[rows, 0:1]
        u = jnp.where(mask, u_row[:, 0:nk], NEG)
        ms = jnp.where(mask, sc, NEG)
        mm = cum + jnp.max(u, axis=1, keepdims=True)
        top = jnp.maximum(jnp.max(ms, axis=1, keepdims=True), mm)
        e = jnp.exp(ms - top)
        d = jnp.exp(u + (cum - top)) * sc
        mml[rows] = jnp.broadcast_to(mm, (CH, 128))
        xs[rows] = jnp.broadcast_to(top, (CH, 128))
        aw[rows] = jnp.broadcast_to(jnp.sum(e, axis=1, keepdims=True), (CH, 128))
        bw[rows] = jnp.broadcast_to(jnp.sum(d, axis=1, keepdims=True), (CH, 128))
        num[rows] = nn((e + d).astype(BF16), v_ref[0:nk, :])

    for i in reversed(range(NCH)):
        chunk_own(i)

    @pl.when(off_diag)
    def _():
        w0.wait()

    def wx_copy(k):
        return remote(
            w_block(z, x), w_block(z, x), wx_s.at[k - 1], wx_r.at[k - 1], (h, z * NX + (x + k) % NX)
        )

    for k in range(1, NX):
        wx_copy(k).start()

    def wait_recv(ref, sem):
        pltpu.make_async_copy(ref, ref, sem).wait()

    wait_recv(meta.at[0 : SEQ - 1], sc_r.at[0])
    wait_recv(crecv.at[0 : (SEQ - 1) * SL], sc_r.at[1])

    def spread(row):
        return jnp.broadcast_to(row, (8, 128))

    def quad(t):
        t = jnp.concatenate([t, t], axis=1)
        return jnp.concatenate([t, t], axis=0)

    def one(i, st):
        p, n, m = st
        csend[piece(i), :] = p.astype(BF16)

        @pl.when(i == s)
        def _():
            carried[:, 0:128] = n
            carried[:, 128:256] = m

        row = meta[i]
        f_i, m_i = spread(row[0:1, :]), spread(row[1:2, :])
        m_new = jnp.maximum(f_i + m, m_i)
        a, b = jnp.exp(f_i + m - m_new), jnp.exp(m_i - m_new)
        p = quad(a) * p + quad(b) * crecv[piece(i), :].astype(F32)
        return p, a * n + b * row, m_new

    lax.fori_loop(
        0,
        SEQ,
        one,
        (jnp.zeros((SL, DV // 2), F32), jnp.zeros((8, 128), F32), jnp.full((8, 128), NEG, F32)),
    )

    def send_prefix(k, c):
        to = (s + k) % SEQ
        remote(csend.at[piece(to)], cpre.at[piece(s)], sc_s.at[2], sc_r.at[2], (h, to)).start()
        return c

    lax.fori_loop(1, SEQ, send_prefix, 0)
    cpre[piece(s), :] = csend[piece(s), :]

    for k in range(1, NX):
        wx_copy(k).wait()

    def wz_copy(step, way):
        dev = (h, (z_up, z_down)[way])
        block = wbuf.at[(z + (NZ - step, step)[way]) % NZ]
        if step == 3:
            block = block.at[pl.ds(way * (DV // 2), DV // 2)]
        return remote(block, block, wz_s.at[way, step], wz_r.at[way, step], dev)

    wz_copy(0, 0).start()
    wz_copy(0, 1).start()

    def wz_next(step):
        for way in (0, 1):
            wz_copy(step - 1, way).wait_recv()
            if step <= 3:
                wz_copy(step, way).start()

    def h_copy(kind, c):
        half = CH // 2
        top, bottom, whole = pl.ds(c * CH, half), pl.ds(c * CH + half, half), pl.ds(c * CH, CH)
        owner, rows, to = {
            "up": (h, whole, up),
            "down": (h, whole, down),
            "mate": (h, whole, mate),
            "up2": (down, top, up),
            "down2": (up, bottom, down),
            "mate_d": (down, whole, mate),
            "mate_u": (up, whole, mate),
            "mate_t": (across, top, mate),
            "mate_b": (across, bottom, mate),
        }[kind]
        k = KINDS.index(kind)
        block = hid.at[owner, rows]
        return remote(block, block, h_s.at[k, c], h_r.at[k, c], (to, s))

    def start(c, *kinds):
        for kind in kinds:
            h_copy(kind, c).start()

    def got(c, *kinds):
        for kind in kinds:
            h_copy(kind, c).wait_recv()

    def chunk_rest(i):
        rows = pl.ds(i * CH, CH)
        nk = ROWS - i * CH
        q = q_ref[rows] * BF16(DK**-0.5)
        sc = nt(q, kp[i * CH : ROWS, :])
        mask = lax.broadcasted_iota(jnp.int32, (CH, nk), 1) > lax.broadcasted_iota(
            jnp.int32, (CH, nk), 0
        )
        mask = jnp.logical_and(mask, s > 0)
        ms = jnp.where(mask, sc, NEG)
        carry = cumc[rows, 0:1] + carried[0:1, 128:129]
        top1 = xs[rows, 0:1]
        top = jnp.maximum(jnp.maximum(top1, jnp.max(ms, axis=1, keepdims=True)), carry)
        e = jnp.exp(ms - top)
        a = jnp.exp(top1 - top)
        cs = jnp.exp(carry - top)
        n_row = jnp.concatenate([carried[2:3, 0:128], carried[3:4, 0:128]], axis=1)
        qn = jnp.sum(q.astype(F32) * n_row, axis=1, keepdims=True)
        den_w = aw[rows, 0:1] * a + jnp.sum(e, axis=1, keepdims=True)
        den_m = bw[rows, 0:1] * a + cs * qn
        floor = jnp.exp(jnp.maximum(mml[rows, 0:1], carry) - top)
        qc = jnp.concatenate([nn(q, cpre[0:DK, :]), nn(q, cpre[DK : 2 * DK, :])], axis=1)
        n = num[rows] * a + nn(e.astype(BF16), vp[i * CH : ROWS, :]) + cs * qc
        hid[h, rows] = (n / (den_w + jnp.maximum(jnp.abs(den_m), floor))).astype(BF16)

    def project(i):
        rows = pl.ds(i * CH, CH)
        acc = nn(hid[0, rows], wbuf[0])
        for b in range(1, HEADS):
            acc = acc + nn(hid[b, rows], wbuf[b])
        out_ref[rows] = acc.astype(BF16)

    def forward1(c):
        got(c, "up", "down")
        start(c, "up2", "down2", "mate_d", "mate_u")

    def forward2(c):
        got(c, "up2", "down2")
        start(c, "mate_t", "mate_b")

    wait_recv(cpre.at[0 : (SEQ - 1) * SL], sc_r.at[2])
    for c in (3, 2, 1, 0):
        for d in kv_copies(c):
            d.wait_recv()
        chunk_rest(c)
        start(c, "up", "down", "mate")
        wz_next({3: 1, 2: 2, 1: 3, 0: 4}[c])
        if c < 3:
            forward1(c + 1)
        if c < 2:
            forward2(c + 2)
    forward1(0)
    forward2(1)
    for c in (3, 2, 1):
        got(c, "mate", "mate_d", "mate_u", "mate_t", "mate_b")
        project(c)
        if c == 3:
            forward2(0)
    got(0, "mate", "mate_d", "mate_u", "mate_t", "mate_b")
    project(0)

    for c in range(NCH):
        for d in kv_copies(c):
            d.wait_send()
        for kind in KINDS:
            h_copy(kind, c).wait_send()
    for step in range(4):
        wz_copy(step, 0).wait_send()
        wz_copy(step, 1).wait_send()
    wait_recv(meta.at[0 : SEQ - 1], sc_s.at[0])
    wait_recv(crecv.at[0 : (SEQ - 1) * SL], sc_s.at[1])
    wait_recv(crecv.at[0 : (SEQ - 1) * SL], sc_s.at[2])


KINDS = ("up", "down", "mate", "up2", "down2", "mate_d", "mate_u", "mate_t", "mate_b")


def local(queries, keys, values, input_gate, forget_gate, out_weight):
    dma = pltpu.SemaphoreType.DMA
    vmem = pl.BlockSpec(memory_space=pltpu.VMEM)
    return pl.pallas_call(
        kernel,
        out_shape=jax.ShapeDtypeStruct((ROWS, DV), BF16),
        in_specs=[vmem] * 6,
        out_specs=vmem,
        scratch_shapes=[
            pltpu.VMEM((ROWS, DK), BF16),
            pltpu.VMEM((ROWS, DV), BF16),
            pltpu.VMEM((HEADS, DV, DV), BF16),
            pltpu.VMEM((HEADS, ROWS, DV), BF16),
            pltpu.VMEM((ROWS, DV), F32),
            pltpu.VMEM((2 * DK, DV // 2), BF16),
            pltpu.VMEM((2 * DK, DV // 2), BF16),
            pltpu.VMEM((2 * DK, DV // 2), BF16),
            pltpu.VMEM((2 * DK, DV // 2), BF16),
            pltpu.VMEM((SEQ, 8, 128), F32),
            pltpu.VMEM((ROWS, 128), F32),
            pltpu.VMEM((ROWS, 128), F32),
            pltpu.VMEM((ROWS, 128), F32),
            pltpu.VMEM((ROWS, 128), F32),
            pltpu.VMEM((ROWS, 128), F32),
            pltpu.VMEM((8, DK), F32),
            dma((NCH, 2)), dma((NCH, 2)),
            dma, dma,
            dma((NX - 1,)), dma((NX - 1,)),
            dma((2, 4)), dma((2, 4)),
            dma((3,)), dma((3,)),
            dma((len(KINDS), NCH)), dma((len(KINDS), NCH)),
        ],
        compiler_params=pltpu.CompilerParams(
            collective_id=0, has_side_effects=True, vmem_limit_bytes=56 << 20
        ),
        cost_estimate=pl.CostEstimate(
            flops=8 * 10**9, bytes_accessed=4 << 20, transcendentals=4 << 20
        ),
    )(queries, keys, values, input_gate.T, forget_gate.T, out_weight)


def solution(mesh):
    placed = (
        P("seq", "head"),
        P("seq", "head"),
        P("seq", "head"),
        P("seq", "head"),
        P("seq", "head"),
        P("head", "seq"),
    )
    return jax.shard_map(
        local, mesh=mesh, in_specs=placed, out_specs=P("seq", "head"), check_vma=False
    )
```

```python
import functools

import jax
import jax.numpy as jnp
from jax import lax
from jax.experimental import pallas as pl
from jax.experimental.pallas import tpu as pltpu
from jax.sharding import PartitionSpec as P

MESH = pl.DeviceIdType.MESH
NEG = -1e30
F32 = jnp.float32
BF16 = jnp.bfloat16

ROWS = 1024
DK = 256
DV = 512
CH = 256
NCH = ROWS // CH
HEADS = 8
SEQ = 32
NZ = 8
NX = 4
QR = 2 * DK // NX
SL = QR // NZ


def nt(a, b):
    return lax.dot_general(a, b, (((1,), (1,)), ((), ())), preferred_element_type=F32)


def nn(a, b):
    return jnp.dot(a, b, preferred_element_type=F32)


def kernel(
    q_ref, k_ref, v_ref, ig_ref, fg_ref, w_ref, out_ref,
    kp, vp, wbuf, hid, num, cflat, cx, ctot, cz, csend, zpre, csend2, cpre, metax, metaz,
    cumc, mml, xs, aw, bw, carried,
    kv_s, kv_r,  w0_s, w0_r, ax_s, ax_r, bz_s, bz_r,
    al_s, al_r, ar_s, ar_r, bl_s, bl_r, br_s, br_r,
    mx_s, mx_r, cx_s, cx_r, px_s, px_r, mz_s, mz_r, cz_s, cz_r, pz_s, pz_r, h_s, h_r,
):
    h = lax.axis_index("head")
    s = lax.axis_index("seq")
    z, x = s // NX, s % NX
    y, core = h // 2, h % 2
    mate = y * 2 + (1 - core)
    up = ((y + 1) % 4) * 2 + core
    down = ((y + 3) % 4) * 2 + core
    across = ((y + 2) % 4) * 2 + core
    z_up = ((z + 1) % NZ) * NX + x
    z_down = ((z + NZ - 1) % NZ) * NX + x

    def remote(src, dst, ss, rs, dev):
        return pltpu.make_async_remote_copy(
            src_ref=src, dst_ref=dst, send_sem=ss, recv_sem=rs, device_id=dev, device_id_type=MESH
        )

    barrier = pltpu.get_barrier_semaphore()

    def greet(dev):
        pl.semaphore_signal(barrier, inc=1, device_id=dev, device_id_type=MESH)

    for k in range(1, NX):
        greet((h, z * NX + (x + k) % NX))
    for k in range(1, NZ):
        greet((h, (z + k) % NZ * NX + x))
    greet((mate, s))
    greet((up, s))
    greet((down, s))
    off_diag = z != h
    first, last = x == 0, x == NX - 1

    @pl.when(off_diag)
    def _():
        greet((z, h * NX + x))

    @pl.when(last)
    def _():
        greet((h, (s + 1) % SEQ))

    @pl.when(first)
    def _():
        greet((h, (s + SEQ - 1) % SEQ))

    greeted = NX - 1 + NZ - 1 + 3 + jnp.where(off_diag, 1, 0) + jnp.where(first | last, 1, 0)

    def kv_copies(c):
        rows = pl.ds(c * CH, CH)
        to = (h, (s + 1) % SEQ)
        return (
            remote(k_ref.at[rows], kp.at[rows], kv_s.at[c, 0], kv_r.at[c, 0], to),
            remote(v_ref.at[rows], vp.at[rows], kv_s.at[c, 1], kv_r.at[c, 1], to),
        )

    def kv_first():
        pass

    def kv_start(c):
        for d in kv_copies(c):
            d.start()

    def w_block(row_block, col):
        return wbuf.at[row_block, :, pl.ds(pl.multiple_of(col * 128, 128), 128)]

    w0 = remote(w_ref, w_block(h, x), w0_s, w0_r, (z, h * NX + x))

    @pl.when(jnp.logical_not(off_diag))
    def _():
        wbuf[z, :, pl.ds(pl.multiple_of(x * 128, 128), 128)] = w_ref[...]

    f_row = fg_ref[...]
    lf = jnp.minimum(f_row, 0.0) - jnp.log1p(jnp.exp(-jnp.abs(f_row)))
    lf8 = jnp.concatenate([lf[:, k * 128 : (k + 1) * 128] for k in range(8)], axis=0)
    tri = (
        lax.broadcasted_iota(jnp.int32, (128, 128), 0)
        <= lax.broadcasted_iota(jnp.int32, (128, 128), 1)
    ).astype(F32)
    part = jnp.dot(lf8, tri, precision=lax.Precision.HIGHEST, preferred_element_type=F32)
    pieces = []
    offset = jnp.zeros((1, 1), F32)
    for k in range(8):
        pieces.append(part[k : k + 1, :] + offset)
        offset = offset + part[k : k + 1, 127:128]
    cum_row = jnp.concatenate(pieces, axis=1)
    total = offset
    u_row = ig_ref[...] - cum_row
    u_max = jnp.max(u_row, axis=1, keepdims=True)
    w_row = jnp.exp(u_row - u_max)
    cumc[...] = jnp.transpose(jnp.broadcast_to(cum_row, (128, ROWS)))
    w_col = jnp.transpose(jnp.broadcast_to(w_row, (128, ROWS)))[:, 0:1]

    kw = k_ref[...].astype(F32) * w_col
    n_own = jnp.sum(kw, axis=0, keepdims=True)
    kw_t = jnp.transpose(kw).astype(BF16)
    cflat[0:DK, :] = nn(kw_t, v_ref[:, 0 : DV // 2]).astype(BF16)
    cflat[DK : 2 * DK, :] = nn(kw_t, v_ref[:, DV // 2 : DV]).astype(BF16)
    metax[x] = jnp.concatenate(
        [
            jnp.broadcast_to(total, (1, 128)),
            jnp.broadcast_to(total + u_max, (1, 128)),
            n_own[:, 0:128],
            n_own[:, 128:256],
            jnp.zeros((4, 128), F32),
        ],
        axis=0,
    )
    pl.semaphore_wait(barrier, greeted)

    def part_of(i, rows):
        return pl.ds(pl.multiple_of(i * rows, rows), rows)

    def to_x(k):
        return (x + k) % NX

    def to_z(k):
        return (z + k) % NZ

    def mx_copy(k):
        dev = (h, z * NX + to_x(k))
        return remote(metax.at[x], metax.at[x], mx_s.at[k - 1], mx_r.at[k - 1], dev)

    def cx_copy(k):
        dev = (h, z * NX + to_x(k))
        return remote(
            cflat.at[part_of(to_x(k), QR)], cx.at[part_of(x, QR)], cx_s.at[k - 1], cx_r.at[k - 1], dev
        )

    def mz_copy(k):
        dev = (h, to_z(k) * NX + x)
        return remote(metaz.at[z], metaz.at[z], mz_s.at[k - 1], mz_r.at[k - 1], dev)

    def cz_copy(k):
        dev = (h, to_z(k) * NX + x)
        return remote(
            ctot.at[part_of(to_z(k), SL)], cz.at[part_of(z, SL)], cz_s.at[k - 1], cz_r.at[k - 1], dev
        )

    def pz_copy(k):
        dev = (h, to_z(k) * NX + x)
        return remote(
            csend.at[part_of(to_z(k), SL)], zpre.at[part_of(z, SL)], pz_s.at[k - 1], pz_r.at[k - 1], dev
        )

    def px_copy(k):
        dev = (h, z * NX + to_x(k))
        return remote(
            csend2.at[part_of(to_x(k), QR)], cpre.at[part_of(x, QR)], px_s.at[k - 1], px_r.at[k - 1], dev
        )

    for k in range(1, NX):
        mx_copy(k).start()
        cx_copy(k).start()
    kv_first()

    @pl.when(off_diag)
    def _():
        w0.start()

    cx[part_of(x, QR), :] = cflat[part_of(x, QR), :]

    def chunk_own(i):
        rows = pl.ds(i * CH, CH)
        nk = (i + 1) * CH
        q = q_ref[rows] * BF16(DK**-0.5)
        sc = nt(q, k_ref[0:nk, :])
        mask = lax.broadcasted_iota(jnp.int32, (CH, nk), 1) <= (
            lax.broadcasted_iota(jnp.int32, (CH, nk), 0) + i * CH
        )
        cum = cumc[rows, 0:1]
        u = jnp.where(mask, u_row[:, 0:nk], NEG)
        ms = jnp.where(mask, sc, NEG)
        mm = cum + jnp.max(u, axis=1, keepdims=True)
        top = jnp.maximum(jnp.max(ms, axis=1, keepdims=True), mm)
        e = jnp.exp(ms - top)
        d = jnp.exp(u + (cum - top)) * sc
        mml[rows] = jnp.broadcast_to(mm, (CH, 128))
        xs[rows] = jnp.broadcast_to(top, (CH, 128))
        aw[rows] = jnp.broadcast_to(jnp.sum(e, axis=1, keepdims=True), (CH, 128))
        bw[rows] = jnp.broadcast_to(jnp.sum(d, axis=1, keepdims=True), (CH, 128))
        num[rows] = nn((e + d).astype(BF16), v_ref[0:nk, :])

    for i in reversed(range(NCH)):
        chunk_own(i)

    half_a, half_b = pl.ds(0, DV // 2), pl.ds(DV // 2, DV // 2)

    def strip(col):
        return pl.ds(pl.multiple_of(col * 128, 128), 128)

    def ax_copy(k):
        piece_a = wbuf.at[z, half_a, strip(x)]
        return remote(piece_a, piece_a, ax_s.at[k - 1], ax_r.at[k - 1], (h, z * NX + (x + k) % NX))

    def bz_copy(k):
        piece_b = wbuf.at[z, half_b, strip(x)]
        return remote(piece_b, piece_b, bz_s.at[k - 1], bz_r.at[k - 1], (h, (z + k) % NZ * NX + x))

    def a_left(step):
        block = wbuf.at[(z + step) % NZ, half_a]
        return remote(block, block, al_s.at[step], al_r.at[step], (h, z_down))

    def a_right(step):
        block = wbuf.at[(z + NZ - step) % NZ, half_a]
        return remote(block, block, ar_s.at[step], ar_r.at[step], (h, z_up))

    def b_left(step):
        block = wbuf.at[:, half_b, strip((x + step) % NX)]
        return remote(block, block, bl_s.at[step], bl_r.at[step], (h, z * NX + (x + NX - 1) % NX))

    def b_right(step):
        block = wbuf.at[:, half_b, strip((x + NX - step) % NX)]
        return remote(block, block, br_s.at[step], br_r.at[step], (h, z * NX + (x + 1) % NX))

    def onward(ring, step):
        if step:
            ring(step - 1).wait_recv()
        ring(step).start()

    def spread(row):
        return jnp.broadcast_to(row, (8, 128))

    def wide(t):
        return jnp.concatenate([t[0:1, :], t[0:1, :]], axis=1)

    def merged(state, tile, block):
        p, n, m = state
        f_i, m_i = spread(tile[0:1, :]), spread(tile[1:2, :])
        m_new = jnp.maximum(f_i + m, m_i)
        a, b = jnp.exp(f_i + m - m_new), jnp.exp(m_i - m_new)
        return wide(a) * p + wide(b) * block.astype(F32), a * n + b * tile, m_new

    for k in range(1, NX):
        mx_copy(k).wait_recv()
        cx_copy(k).wait_recv()
    empty = jnp.zeros((8, 128), F32), jnp.full((8, 128), NEG, F32)
    state = (jnp.zeros((QR, DV // 2), F32), *empty)
    decay = jnp.zeros((8, 128), F32)
    for i in range(NX):
        tile = metax[i]
        state = merged(state, tile, cx[i * QR : (i + 1) * QR, :])
        decay = decay + spread(tile[0:1, :])
    ctot[...] = state[0].astype(BF16)
    line = lax.broadcasted_iota(jnp.int32, (8, 128), 0)
    metaz[z] = jnp.where(line == 0, decay, jnp.where(line == 1, state[2], state[1]))
    for k in range(1, NZ):
        mz_copy(k).start()
        cz_copy(k).start()
    cz[part_of(z, SL), :] = ctot[part_of(z, SL), :]

    @pl.when(off_diag)
    def _():
        w0.wait()

    for k in range(1, NX):
        ax_copy(k).start()

    for k in range(1, NZ):
        mz_copy(k).wait_recv()
        cz_copy(k).wait_recv()
    state = (jnp.zeros((SL, DV // 2), F32), *empty)
    for i in range(NZ):
        csend[i * SL : (i + 1) * SL, :] = state[0].astype(BF16)

        @pl.when(z == i)
        def _():
            carried[:, 0:128] = state[1]
            carried[:, 128:256] = state[2]

        if i < NZ - 1:
            state = merged(state, metaz[i], cz[i * SL : (i + 1) * SL, :])
    for k in range(1, NZ):
        pz_copy(k).start()
    zpre[part_of(z, SL), :] = csend[part_of(z, SL), :]
    for k in range(1, NZ):
        bz_copy(k).start()
    for k in range(1, NZ):
        pz_copy(k).wait_recv()
    state = (zpre[...].astype(F32), carried[:, 0:128], carried[:, 128:256])
    for i in range(NX):
        csend2[i * QR : (i + 1) * QR, :] = state[0].astype(BF16)

        @pl.when(x == i)
        def _():
            carried[:, 0:128] = state[1]
            carried[:, 128:256] = state[2]

        if i < NX - 1:
            state = merged(state, metax[i], cx[i * QR : (i + 1) * QR, :])
    for k in range(1, NX):
        px_copy(k).start()
    kv_start(3)
    kv_start(2)
    kv_start(1)
    kv_start(0)
    cpre[part_of(x, QR), :] = csend2[part_of(x, QR), :]

    def h_copy(kind, c):
        half = CH // 2
        top, bottom, whole = pl.ds(c * CH, half), pl.ds(c * CH + half, half), pl.ds(c * CH, CH)
        owner, rows, to = {
            "up": (h, whole, up),
            "down": (h, whole, down),
            "mate": (h, whole, mate),
            "up2": (down, top, up),
            "down2": (up, bottom, down),
            "mate_d": (down, whole, mate),
            "mate_u": (up, whole, mate),
            "mate_t": (across, top, mate),
            "mate_b": (across, bottom, mate),
        }[kind]
        k = KINDS.index(kind)
        block = hid.at[owner, rows]
        return remote(block, block, h_s.at[k, c], h_r.at[k, c], (to, s))

    def start(c, *kinds):
        for kind in kinds:
            h_copy(kind, c).start()

    def got(c, *kinds):
        for kind in kinds:
            h_copy(kind, c).wait_recv()

    def chunk_rest(i):
        rows = pl.ds(i * CH, CH)
        nk = ROWS - i * CH
        q = q_ref[rows] * BF16(DK**-0.5)
        sc = nt(q, kp[i * CH : ROWS, :])
        mask = lax.broadcasted_iota(jnp.int32, (CH, nk), 1) > lax.broadcasted_iota(
            jnp.int32, (CH, nk), 0
        )
        mask = jnp.logical_and(mask, s > 0)
        ms = jnp.where(mask, sc, NEG)
        carry = cumc[rows, 0:1] + carried[0:1, 128:129]
        top1 = xs[rows, 0:1]
        top = jnp.maximum(jnp.maximum(top1, jnp.max(ms, axis=1, keepdims=True)), carry)
        e = jnp.exp(ms - top)
        a = jnp.exp(top1 - top)
        cs = jnp.exp(carry - top)
        n_row = jnp.concatenate([carried[2:3, 0:128], carried[3:4, 0:128]], axis=1)
        qn = jnp.sum(q.astype(F32) * n_row, axis=1, keepdims=True)
        den_w = aw[rows, 0:1] * a + jnp.sum(e, axis=1, keepdims=True)
        den_m = bw[rows, 0:1] * a + cs * qn
        floor = jnp.exp(jnp.maximum(mml[rows, 0:1], carry) - top)
        qc = jnp.concatenate([nn(q, cpre[0:DK, :]), nn(q, cpre[DK : 2 * DK, :])], axis=1)
        n = num[rows] * a + nn(e.astype(BF16), vp[i * CH : ROWS, :]) + cs * qc
        hid[h, rows] = (n / (den_w + jnp.maximum(jnp.abs(den_m), floor))).astype(BF16)

    def project(i):
        rows = pl.ds(i * CH, CH)
        acc = nn(hid[0, rows], wbuf[0])
        for b in range(1, HEADS):
            acc = acc + nn(hid[b, rows], wbuf[b])
        out_ref[rows] = acc.astype(BF16)

    def forward1(c):
        got(c, "up", "down")
        start(c, "up2", "down2", "mate_d", "mate_u")

    def forward2(c):
        got(c, "up2", "down2")
        start(c, "mate_t", "mate_b")

    def hidden(c):
        for d in kv_copies(c):
            d.wait_recv()
        chunk_rest(c)
        start(c, "up", "down", "mate")

    for k in range(1, NX):
        ax_copy(k).wait_recv()
    onward(a_left, 0)
    for k in range(1, NX):
        px_copy(k).wait_recv()
    hidden(3)
    for k in range(1, NZ):
        bz_copy(k).wait_recv()
    onward(b_left, 0)
    onward(a_right, 0)
    hidden(2)
    forward1(3)
    onward(a_left, 1)
    forward2(3)
    hidden(1)
    onward(b_right, 0)
    forward1(2)
    onward(b_left, 1)
    onward(a_left, 2)
    forward2(2)
    hidden(0)
    forward1(1)
    onward(a_right, 1)
    onward(a_left, 3)
    forward2(1)
    forward1(0)
    onward(a_left, 4)
    a_right(1).wait_recv()
    b_left(1).wait_recv()
    b_right(0).wait_recv()
    forward2(0)
    a_left(4).wait_recv()
    for c in (3, 2, 1, 0):
        got(c, "mate", "mate_d", "mate_u", "mate_t", "mate_b")
        project(c)

    for c in range(NCH):
        for d in kv_copies(c):
            d.wait_send()

    for c in range(NCH):
        for kind in KINDS:
            h_copy(kind, c).wait_send()
    for ring, steps in ((a_left, 5), (a_right, 2), (b_left, 2), (b_right, 1)):
        for step in range(steps):
            ring(step).wait_send()
    for k in range(1, NX):
        ax_copy(k).wait_send()
    for k in range(1, NZ):
        bz_copy(k).wait_send()
    for k in range(1, NX):
        mx_copy(k).wait_send()
        cx_copy(k).wait_send()
        px_copy(k).wait_send()
    for k in range(1, NZ):
        mz_copy(k).wait_send()
        cz_copy(k).wait_send()
        pz_copy(k).wait_send()


KINDS = ("up", "down", "mate", "up2", "down2", "mate_d", "mate_u", "mate_t", "mate_b")


def local(queries, keys, values, input_gate, forget_gate, out_weight):
    dma = pltpu.SemaphoreType.DMA
    vmem = pl.BlockSpec(memory_space=pltpu.VMEM)
    return pl.pallas_call(
        kernel,
        out_shape=jax.ShapeDtypeStruct((ROWS, DV), BF16),
        in_specs=[vmem] * 6,
        out_specs=vmem,
        scratch_shapes=[
            pltpu.VMEM((ROWS, DK), BF16),
            pltpu.VMEM((ROWS, DV), BF16),
            pltpu.VMEM((HEADS, DV, DV), BF16),
            pltpu.VMEM((HEADS, ROWS, DV), BF16),
            pltpu.VMEM((ROWS, DV), F32),
            pltpu.VMEM((2 * DK, DV // 2), BF16),
            pltpu.VMEM((2 * DK, DV // 2), BF16),
            pltpu.VMEM((QR, DV // 2), BF16),
            pltpu.VMEM((QR, DV // 2), BF16),
            pltpu.VMEM((QR, DV // 2), BF16),
            pltpu.VMEM((QR, DV // 2), BF16),
            pltpu.VMEM((2 * DK, DV // 2), BF16),
            pltpu.VMEM((2 * DK, DV // 2), BF16),
            pltpu.VMEM((NX, 8, 128), F32),
            pltpu.VMEM((NZ, 8, 128), F32),
            pltpu.VMEM((ROWS, 128), F32),
            pltpu.VMEM((ROWS, 128), F32),
            pltpu.VMEM((ROWS, 128), F32),
            pltpu.VMEM((ROWS, 128), F32),
            pltpu.VMEM((ROWS, 128), F32),
            pltpu.VMEM((8, DK), F32),
            dma((NCH, 2)), dma((NCH, 2)),
            dma, dma,
            dma((NX - 1,)), dma((NX - 1,)),
            dma((NZ - 1,)), dma((NZ - 1,)),
            dma((5,)), dma((5,)),
            dma((2,)), dma((2,)),
            dma((2,)), dma((2,)),
            dma((1,)), dma((1,)),
            *[dma((NX - 1,))] * 6,
            *[dma((NZ - 1,))] * 6,
            dma((len(KINDS), NCH)), dma((len(KINDS), NCH)),
        ],
        compiler_params=pltpu.CompilerParams(
            collective_id=0, has_side_effects=True, vmem_limit_bytes=56 << 20
        ),
        cost_estimate=pl.CostEstimate(
            flops=8 * 10**9, bytes_accessed=4 << 20, transcendentals=4 << 20
        ),
    )(queries, keys, values, input_gate.T, forget_gate.T, out_weight)


def solution(mesh):
    placed = (
        P("seq", "head"),
        P("seq", "head"),
        P("seq", "head"),
        P("seq", "head"),
        P("seq", "head"),
        P("head", "seq"),
    )
    return jax.shard_map(
        local, mesh=mesh, in_specs=placed, out_specs=P("seq", "head"), check_vma=False
    )
```

```python
import functools

import jax
import jax.numpy as jnp
from jax import lax
from jax.experimental import pallas as pl
from jax.experimental.pallas import tpu as pltpu
from jax.sharding import PartitionSpec as P

MESH = pl.DeviceIdType.MESH
NEG = -1e30
F32 = jnp.float32
BF16 = jnp.bfloat16

ROWS = 1024
DK = 256
DV = 512
CH = 256
NCH = ROWS // CH
HEADS = 8
SEQ = 32
NZ = 8
NX = 4
QR = 2 * DK // NX
SL = QR // NZ


def nt(a, b):
    return lax.dot_general(a, b, (((1,), (1,)), ((), ())), preferred_element_type=F32)


def nn(a, b):
    return jnp.dot(a, b, preferred_element_type=F32)


def kernel(
    q_ref, k_ref, v_ref, ig_ref, fg_ref, w_ref, out_ref,
    kp, vp, wbuf, hid, num, cflat, cx, ctot, cz, csend, zpre, csend2, cpre, metax, metaz,
    cumc, mml, xs, aw, bw, carried,
    kv_s, kv_r,  w0_s, w0_r, ax_s, ax_r, bz_s, bz_r,
    al_s, al_r, ar_s, ar_r, bl_s, bl_r, br_s, br_r,
    mx_s, mx_r, cx_s, cx_r, px_s, px_r, mz_s, mz_r, cz_s, cz_r, pz_s, pz_r, h_s, h_r,
):
    h = lax.axis_index("head")
    s = lax.axis_index("seq")
    z, x = s // NX, s % NX
    y, core = h // 2, h % 2
    mate = y * 2 + (1 - core)
    up = ((y + 1) % 4) * 2 + core
    down = ((y + 3) % 4) * 2 + core
    across = ((y + 2) % 4) * 2 + core
    z_up = ((z + 1) % NZ) * NX + x
    z_down = ((z + NZ - 1) % NZ) * NX + x

    def remote(src, dst, ss, rs, dev):
        return pltpu.make_async_remote_copy(
            src_ref=src, dst_ref=dst, send_sem=ss, recv_sem=rs, device_id=dev, device_id_type=MESH
        )

    barrier = pltpu.get_barrier_semaphore()

    def greet(dev):
        pl.semaphore_signal(barrier, inc=1, device_id=dev, device_id_type=MESH)

    for k in range(1, NX):
        greet((h, z * NX + (x + k) % NX))
    for k in range(1, NZ):
        greet((h, (z + k) % NZ * NX + x))
    greet((mate, s))
    greet((up, s))
    greet((down, s))
    off_diag = z != h
    first, last = x == 0, x == NX - 1

    @pl.when(off_diag)
    def _():
        greet((z, h * NX + x))

    @pl.when(last)
    def _():
        greet((h, (s + 1) % SEQ))

    @pl.when(first)
    def _():
        greet((h, (s + SEQ - 1) % SEQ))

    greeted = NX - 1 + NZ - 1 + 3 + jnp.where(off_diag, 1, 0) + jnp.where(first | last, 1, 0)

    def kv_copies(c):
        rows = pl.ds(c * CH, CH)
        to = (h, (s + 1) % SEQ)
        return (
            remote(k_ref.at[rows], kp.at[rows], kv_s.at[c, 0], kv_r.at[c, 0], to),
            remote(v_ref.at[rows], vp.at[rows], kv_s.at[c, 1], kv_r.at[c, 1], to),
        )

    def kv_first():
        pass

    def kv_start(c):
        for d in kv_copies(c):
            d.start()

    def w_block(row_block, col):
        return wbuf.at[row_block, :, pl.ds(pl.multiple_of(col * 128, 128), 128)]

    w0 = remote(w_ref, w_block(h, x), w0_s, w0_r, (z, h * NX + x))

    @pl.when(jnp.logical_not(off_diag))
    def _():
        wbuf[z, :, pl.ds(pl.multiple_of(x * 128, 128), 128)] = w_ref[...]

    f_row = fg_ref[...]
    lf = jnp.minimum(f_row, 0.0) - jnp.log1p(jnp.exp(-jnp.abs(f_row)))
    lf8 = jnp.concatenate([lf[:, k * 128 : (k + 1) * 128] for k in range(8)], axis=0)
    tri = (
        lax.broadcasted_iota(jnp.int32, (128, 128), 0)
        <= lax.broadcasted_iota(jnp.int32, (128, 128), 1)
    ).astype(F32)
    part = jnp.dot(lf8, tri, precision=lax.Precision.HIGHEST, preferred_element_type=F32)
    pieces = []
    offset = jnp.zeros((1, 1), F32)
    for k in range(8):
        pieces.append(part[k : k + 1, :] + offset)
        offset = offset + part[k : k + 1, 127:128]
    cum_row = jnp.concatenate(pieces, axis=1)
    total = offset
    u_row = ig_ref[...] - cum_row
    u_max = jnp.max(u_row, axis=1, keepdims=True)
    w_row = jnp.exp(u_row - u_max)
    cumc[...] = jnp.transpose(jnp.broadcast_to(cum_row, (128, ROWS)))
    w_col = jnp.transpose(jnp.broadcast_to(w_row, (128, ROWS)))[:, 0:1]

    kw = k_ref[...].astype(F32) * w_col
    n_own = jnp.sum(kw, axis=0, keepdims=True)
    kw_t = jnp.transpose(kw).astype(BF16)
    cflat[0:DK, :] = nn(kw_t, v_ref[:, 0 : DV // 2]).astype(BF16)
    cflat[DK : 2 * DK, :] = nn(kw_t, v_ref[:, DV // 2 : DV]).astype(BF16)
    metax[x] = jnp.concatenate(
        [
            jnp.broadcast_to(total, (1, 128)),
            jnp.broadcast_to(total + u_max, (1, 128)),
            n_own[:, 0:128],
            n_own[:, 128:256],
            jnp.zeros((4, 128), F32),
        ],
        axis=0,
    )
    pl.semaphore_wait(barrier, greeted)

    def part_of(i, rows):
        return pl.ds(pl.multiple_of(i * rows, rows), rows)

    def to_x(k):
        return (x + k) % NX

    def to_z(k):
        return (z + k) % NZ

    def mx_copy(k):
        dev = (h, z * NX + to_x(k))
        return remote(metax.at[x], metax.at[x], mx_s.at[k - 1], mx_r.at[k - 1], dev)

    def cx_copy(k):
        dev = (h, z * NX + to_x(k))
        return remote(
            cflat.at[part_of(to_x(k), QR)], cx.at[part_of(x, QR)], cx_s.at[k - 1], cx_r.at[k - 1], dev
        )

    def mz_copy(k):
        dev = (h, to_z(k) * NX + x)
        return remote(metaz.at[z], metaz.at[z], mz_s.at[k - 1], mz_r.at[k - 1], dev)

    def cz_copy(k):
        dev = (h, to_z(k) * NX + x)
        return remote(
            ctot.at[part_of(to_z(k), SL)], cz.at[part_of(z, SL)], cz_s.at[k - 1], cz_r.at[k - 1], dev
        )

    def pz_copy(k):
        dev = (h, to_z(k) * NX + x)
        return remote(
            csend.at[part_of(to_z(k), SL)], zpre.at[part_of(z, SL)], pz_s.at[k - 1], pz_r.at[k - 1], dev
        )

    def px_copy(k):
        dev = (h, z * NX + to_x(k))
        return remote(
            csend2.at[part_of(to_x(k), QR)], cpre.at[part_of(x, QR)], px_s.at[k - 1], px_r.at[k - 1], dev
        )

    for k in range(1, NX):
        mx_copy(k).start()
        cx_copy(k).start()
    kv_first()

    @pl.when(off_diag)
    def _():
        w0.start()

    cx[part_of(x, QR), :] = cflat[part_of(x, QR), :]

    def chunk_own(i):
        rows = pl.ds(i * CH, CH)
        nk = (i + 1) * CH
        q = q_ref[rows] * BF16(DK**-0.5)
        sc = nt(q, k_ref[0:nk, :])
        mask = lax.broadcasted_iota(jnp.int32, (CH, nk), 1) <= (
            lax.broadcasted_iota(jnp.int32, (CH, nk), 0) + i * CH
        )
        cum = cumc[rows, 0:1]
        u = jnp.where(mask, u_row[:, 0:nk], NEG)
        ms = jnp.where(mask, sc, NEG)
        mm = cum + jnp.max(u, axis=1, keepdims=True)
        top = jnp.maximum(jnp.max(ms, axis=1, keepdims=True), mm)
        e = jnp.exp(ms - top)
        d = jnp.exp(u + (cum - top)) * sc
        mml[rows] = jnp.broadcast_to(mm, (CH, 128))
        xs[rows] = jnp.broadcast_to(top, (CH, 128))
        aw[rows] = jnp.broadcast_to(jnp.sum(e, axis=1, keepdims=True), (CH, 128))
        bw[rows] = jnp.broadcast_to(jnp.sum(d, axis=1, keepdims=True), (CH, 128))
        num[rows] = nn((e + d).astype(BF16), v_ref[0:nk, :])

    for i in reversed(range(NCH)):
        chunk_own(i)

    half_a, half_b = pl.ds(0, DV // 2), pl.ds(DV // 2, DV // 2)

    def strip(col):
        return pl.ds(pl.multiple_of(col * 128, 128), 128)

    def ax_copy(k):
        piece_a = wbuf.at[z, half_a, strip(x)]
        return remote(piece_a, piece_a, ax_s.at[k - 1], ax_r.at[k - 1], (h, z * NX + (x + k) % NX))

    def bz_copy(k):
        piece_b = wbuf.at[z, half_b, strip(x)]
        return remote(piece_b, piece_b, bz_s.at[k - 1], bz_r.at[k - 1], (h, (z + k) % NZ * NX + x))

    def a_left(step):
        block = wbuf.at[(z + step) % NZ, half_a]
        return remote(block, block, al_s.at[step], al_r.at[step], (h, z_down))

    def a_right(step):
        block = wbuf.at[(z + NZ - step) % NZ, half_a]
        return remote(block, block, ar_s.at[step], ar_r.at[step], (h, z_up))

    def b_left(step):
        block = wbuf.at[:, half_b, strip((x + step) % NX)]
        return remote(block, block, bl_s.at[step], bl_r.at[step], (h, z * NX + (x + NX - 1) % NX))

    def b_right(step):
        block = wbuf.at[:, half_b, strip((x + NX - step) % NX)]
        return remote(block, block, br_s.at[step], br_r.at[step], (h, z * NX + (x + 1) % NX))

    def onward(ring, step):
        if step:
            ring(step - 1).wait_recv()
        ring(step).start()

    def spread(row):
        return jnp.broadcast_to(row, (8, 128))

    def wide(t):
        return jnp.concatenate([t[0:1, :], t[0:1, :]], axis=1)

    def merged(state, tile, block):
        p, n, m = state
        f_i, m_i = spread(tile[0:1, :]), spread(tile[1:2, :])
        m_new = jnp.maximum(f_i + m, m_i)
        a, b = jnp.exp(f_i + m - m_new), jnp.exp(m_i - m_new)
        return wide(a) * p + wide(b) * block.astype(F32), a * n + b * tile, m_new

    for k in range(1, NX):
        mx_copy(k).wait_recv()
        cx_copy(k).wait_recv()
    empty = jnp.zeros((8, 128), F32), jnp.full((8, 128), NEG, F32)
    state = (jnp.zeros((QR, DV // 2), F32), *empty)
    decay = jnp.zeros((8, 128), F32)
    for i in range(NX):
        tile = metax[i]
        state = merged(state, tile, cx[i * QR : (i + 1) * QR, :])
        decay = decay + spread(tile[0:1, :])
    ctot[...] = state[0].astype(BF16)
    line = lax.broadcasted_iota(jnp.int32, (8, 128), 0)
    metaz[z] = jnp.where(line == 0, decay, jnp.where(line == 1, state[2], state[1]))
    for k in range(1, NZ):
        mz_copy(k).start()
        cz_copy(k).start()
    cz[part_of(z, SL), :] = ctot[part_of(z, SL), :]

    @pl.when(off_diag)
    def _():
        w0.wait()

    for k in range(1, NX):
        ax_copy(k).start()

    for k in range(1, NZ):
        mz_copy(k).wait_recv()
        cz_copy(k).wait_recv()
    state = (jnp.zeros((SL, DV // 2), F32), *empty)
    for i in range(NZ):
        csend[i * SL : (i + 1) * SL, :] = state[0].astype(BF16)

        @pl.when(z == i)
        def _():
            carried[:, 0:128] = state[1]
            carried[:, 128:256] = state[2]

        if i < NZ - 1:
            state = merged(state, metaz[i], cz[i * SL : (i + 1) * SL, :])
    for k in range(1, NZ):
        pz_copy(k).start()
    zpre[part_of(z, SL), :] = csend[part_of(z, SL), :]
    for k in range(1, NZ):
        bz_copy(k).start()
    for k in range(1, NZ):
        pz_copy(k).wait_recv()
    state = (zpre[...].astype(F32), carried[:, 0:128], carried[:, 128:256])
    for i in range(NX):
        csend2[i * QR : (i + 1) * QR, :] = state[0].astype(BF16)

        @pl.when(x == i)
        def _():
            carried[:, 0:128] = state[1]
            carried[:, 128:256] = state[2]

        if i < NX - 1:
            state = merged(state, metax[i], cx[i * QR : (i + 1) * QR, :])
    for k in range(1, NX):
        px_copy(k).start()
    kv_start(3)
    kv_start(2)
    kv_start(1)
    kv_start(0)
    cpre[part_of(x, QR), :] = csend2[part_of(x, QR), :]

    def h_copy(kind, c):
        half = CH // 2
        top, bottom, whole = pl.ds(c * CH, half), pl.ds(c * CH + half, half), pl.ds(c * CH, CH)
        owner, rows, to = {
            "up": (h, whole, up),
            "down": (h, whole, down),
            "mate": (h, whole, mate),
            "up2": (down, top, up),
            "down2": (up, bottom, down),
            "mate_d": (down, whole, mate),
            "mate_u": (up, whole, mate),
            "mate_t": (across, top, mate),
            "mate_b": (across, bottom, mate),
        }[kind]
        k = KINDS.index(kind)
        block = hid.at[owner, rows]
        return remote(block, block, h_s.at[k, c], h_r.at[k, c], (to, s))

    def start(c, *kinds):
        for kind in kinds:
            h_copy(kind, c).start()

    def got(c, *kinds):
        for kind in kinds:
            h_copy(kind, c).wait_recv()

    def chunk_rest(i):
        rows = pl.ds(i * CH, CH)
        nk = ROWS - i * CH
        q = q_ref[rows] * BF16(DK**-0.5)
        sc = nt(q, kp[i * CH : ROWS, :])
        mask = lax.broadcasted_iota(jnp.int32, (CH, nk), 1) > lax.broadcasted_iota(
            jnp.int32, (CH, nk), 0
        )
        mask = jnp.logical_and(mask, s > 0)
        ms = jnp.where(mask, sc, NEG)
        carry = cumc[rows, 0:1] + carried[0:1, 128:129]
        top1 = xs[rows, 0:1]
        top = jnp.maximum(jnp.maximum(top1, jnp.max(ms, axis=1, keepdims=True)), carry)
        e = jnp.exp(ms - top)
        a = jnp.exp(top1 - top)
        cs = jnp.exp(carry - top)
        n_row = jnp.concatenate([carried[2:3, 0:128], carried[3:4, 0:128]], axis=1)
        qn = jnp.sum(q.astype(F32) * n_row, axis=1, keepdims=True)
        den_w = aw[rows, 0:1] * a + jnp.sum(e, axis=1, keepdims=True)
        den_m = bw[rows, 0:1] * a + cs * qn
        floor = jnp.exp(jnp.maximum(mml[rows, 0:1], carry) - top)
        qc = jnp.concatenate([nn(q, cpre[0:DK, :]), nn(q, cpre[DK : 2 * DK, :])], axis=1)
        n = num[rows] * a + nn(e.astype(BF16), vp[i * CH : ROWS, :]) + cs * qc
        hid[h, rows] = (n / (den_w + jnp.maximum(jnp.abs(den_m), floor))).astype(BF16)

    late = (z + 5) % NZ

    def project(i):
        rows = pl.ds(i * CH, CH)
        acc = nn(hid[late, rows, DV // 2 : DV], wbuf[late, DV // 2 : DV, :])
        for k in (0, 1, 2, 3, 4, 6, 7):
            b = (z + k) % NZ
            acc = acc + nn(hid[b, rows], wbuf[b])
        num[rows] = acc

    def finish(i):
        rows = pl.ds(i * CH, CH)
        out_ref[rows] = (
            num[rows] + nn(hid[late, rows, 0 : DV // 2], wbuf[late, 0 : DV // 2, :])
        ).astype(BF16)

    def forward1(c):
        got(c, "up", "down")
        start(c, "up2", "down2", "mate_d", "mate_u")

    def forward2(c):
        got(c, "up2", "down2")
        start(c, "mate_t", "mate_b")

    def hidden(c):
        for d in kv_copies(c):
            d.wait_recv()
        chunk_rest(c)
        start(c, "up", "down", "mate")

    for k in range(1, NX):
        ax_copy(k).wait_recv()
    onward(a_left, 0)
    for k in range(1, NX):
        px_copy(k).wait_recv()
    hidden(3)
    for k in range(1, NZ):
        bz_copy(k).wait_recv()
    onward(b_left, 0)
    onward(a_right, 0)
    hidden(2)
    forward1(3)
    onward(a_left, 1)
    forward2(3)
    hidden(1)
    onward(b_right, 0)
    forward1(2)
    onward(b_left, 1)
    onward(a_left, 2)
    forward2(2)
    hidden(0)
    forward1(1)
    onward(a_right, 1)
    onward(a_left, 3)
    forward2(1)
    forward1(0)
    onward(a_left, 4)
    a_right(1).wait_recv()
    b_left(1).wait_recv()
    b_right(0).wait_recv()
    forward2(0)
    for c in (3, 2, 1, 0):
        got(c, "mate", "mate_d", "mate_u", "mate_t", "mate_b")
        project(c)
    a_left(4).wait_recv()
    for c in (3, 2, 1, 0):
        finish(c)

    for c in range(NCH):
        for d in kv_copies(c):
            d.wait_send()

    for c in range(NCH):
        for kind in KINDS:
            h_copy(kind, c).wait_send()
    for ring, steps in ((a_left, 5), (a_right, 2), (b_left, 2), (b_right, 1)):
        for step in range(steps):
            ring(step).wait_send()
    for k in range(1, NX):
        ax_copy(k).wait_send()
    for k in range(1, NZ):
        bz_copy(k).wait_send()
    for k in range(1, NX):
        mx_copy(k).wait_send()
        cx_copy(k).wait_send()
        px_copy(k).wait_send()
    for k in range(1, NZ):
        mz_copy(k).wait_send()
        cz_copy(k).wait_send()
        pz_copy(k).wait_send()


KINDS = ("up", "down", "mate", "up2", "down2", "mate_d", "mate_u", "mate_t", "mate_b")


def local(queries, keys, values, input_gate, forget_gate, out_weight):
    dma = pltpu.SemaphoreType.DMA
    vmem = pl.BlockSpec(memory_space=pltpu.VMEM)
    return pl.pallas_call(
        kernel,
        out_shape=jax.ShapeDtypeStruct((ROWS, DV), BF16),
        in_specs=[vmem] * 6,
        out_specs=vmem,
        scratch_shapes=[
            pltpu.VMEM((ROWS, DK), BF16),
            pltpu.VMEM((ROWS, DV), BF16),
            pltpu.VMEM((HEADS, DV, DV), BF16),
            pltpu.VMEM((HEADS, ROWS, DV), BF16),
            pltpu.VMEM((ROWS, DV), F32),
            pltpu.VMEM((2 * DK, DV // 2), BF16),
            pltpu.VMEM((2 * DK, DV // 2), BF16),
            pltpu.VMEM((QR, DV // 2), BF16),
            pltpu.VMEM((QR, DV // 2), BF16),
            pltpu.VMEM((QR, DV // 2), BF16),
            pltpu.VMEM((QR, DV // 2), BF16),
            pltpu.VMEM((2 * DK, DV // 2), BF16),
            pltpu.VMEM((2 * DK, DV // 2), BF16),
            pltpu.VMEM((NX, 8, 128), F32),
            pltpu.VMEM((NZ, 8, 128), F32),
            pltpu.VMEM((ROWS, 128), F32),
            pltpu.VMEM((ROWS, 128), F32),
            pltpu.VMEM((ROWS, 128), F32),
            pltpu.VMEM((ROWS, 128), F32),
            pltpu.VMEM((ROWS, 128), F32),
            pltpu.VMEM((8, DK), F32),
            dma((NCH, 2)), dma((NCH, 2)),
            dma, dma,
            dma((NX - 1,)), dma((NX - 1,)),
            dma((NZ - 1,)), dma((NZ - 1,)),
            dma((5,)), dma((5,)),
            dma((2,)), dma((2,)),
            dma((2,)), dma((2,)),
            dma((1,)), dma((1,)),
            *[dma((NX - 1,))] * 6,
            *[dma((NZ - 1,))] * 6,
            dma((len(KINDS), NCH)), dma((len(KINDS), NCH)),
        ],
        compiler_params=pltpu.CompilerParams(
            collective_id=0, has_side_effects=True, vmem_limit_bytes=56 << 20
        ),
        cost_estimate=pl.CostEstimate(
            flops=8 * 10**9, bytes_accessed=4 << 20, transcendentals=4 << 20
        ),
    )(queries, keys, values, input_gate.T, forget_gate.T, out_weight)


def solution(mesh):
    placed = (
        P("seq", "head"),
        P("seq", "head"),
        P("seq", "head"),
        P("seq", "head"),
        P("seq", "head"),
        P("head", "seq"),
    )
    return jax.shard_map(
        local, mesh=mesh, in_specs=placed, out_specs=P("seq", "head"), check_vma=False
    )
```
